32 devices in a mesh: context: 8 (over z, y), tensor: 4 (over x, core).
Axes of the slice: x: 2, y: 2, z: 4, core: 2. Of those that a mesh axis runs over, the one named last changes fastest.
Arguments:
- qkv: bfloat16 [8192, 3, 2048], P('context', None, 'tensor'), may hold values from -6 to 6
- short_filter: float32 [7, 3, 2048], P(None, None, 'tensor'), may hold values from -2 to 2
- long_filter: float32 [128, 2048], P(None, 'tensor'), may hold values from -0.5 to 0.5
- out_weight: bfloat16 [2048, 2048], P('tensor'), may hold values from -0.125 to 0.125
- out_grad: bfloat16 [8192, 2048], P('context'), may hold values from -6 to 6
Outputs:
- output: bfloat16 [8192, 2048], P('context')
- qkv_grad: bfloat16 [8192, 3, 2048], P('context', None, 'tensor')
- long_grad: float32 [128, 2048], P(None, 'tensor')
- short_grad: float32 [7, 3, 2048], P(None, None, 'tensor')
- weight_grad: float32 [2048, 2048], P('context', 'tensor')
The draws below stay inside these ranges and needn't reach their ends.
All inputs are finite; a program needn't handle non-finite values.
Results may differ from the reference program's by a relative error of at most 0.009.
Values may be sent and summed in bfloat16 or wider, within the bound.
A program may use at most 128 MiB of HBM per device.

```python
import jax
import jax.numpy as jnp
from jax import lax

D = 2048
LONG = 128
SHORT = 7
TOKENS = 8192
N_TENSOR = 4


def raised(array, key, source, target, blocks, factor):
    def block_of(position):
        return (jnp.arange(array.shape[position]) // (array.shape[position] // blocks)).reshape((-1,) + (1,) * (array.ndim - 1 - position))

    near = jax.random.permutation(key, blocks)[block_of(target)]
    second = (block_of(target) + blocks // 2) % blocks
    return jnp.where((block_of(source) == near) | (block_of(source) == second), factor * array, array)


def block_levels(own_key, shape, pieces, smallest, high):
    gain, own = 1.0, jax.random.fold_in(own_key, 6)
    for position, shards_of in pieces:
        draws = jnp.exp(jax.random.uniform(jax.random.fold_in(own, position), (shards_of,), jnp.float32, smallest / len(pieces), high / len(pieces)))
        gain = gain * jnp.repeat(draws, shape[position] // shards_of).reshape([-1 if axis == position else 1 for axis in range(len(shape))])
    return gain


def bell_draw(rng, dims, spread, most, split=(), held_as=jnp.bfloat16):
    gain = block_levels(rng, dims, split, -0.22, 0.18) if split else 1.0
    drawn = jax.random.normal(rng, dims, jnp.float32) * spread * gain
    return jnp.minimum(jnp.maximum(drawn, -most), most).astype(held_as)


def bell_draw_with(key, shape, scale, reach, shards, heavy, dtype=jnp.bfloat16):
    entries = scale * jax.random.normal(key, shape, jnp.float32)
    if shards:
        entries = entries * block_levels(key, shape, shards, -0.22, 0.18)
    return jnp.clip(raised(entries, jax.random.fold_in(key, 3), *heavy), -reach, reach).astype(dtype)


def setup_inputs(seed: int = 0) -> dict:
    streams_of = jax.random.split(jax.random.key(seed), 6)
    qkv = bell_draw(streams_of[0], (TOKENS, 3, D), 1.0, 6.0, ((0, 8), (2, 4)))
    short_filter = bell_draw(streams_of[1], (SHORT, 3, D), SHORT ** -0.5, 2.0, ((2, 4),), jnp.float32)
    long_filter = bell_draw(streams_of[2], (LONG, D), LONG ** -0.5, 0.5, ((1, 4),), jnp.float32)
    out_weight = bell_draw(streams_of[3], (D, D), D ** -0.5, 0.125, ((0, 4),))
    out_grad = bell_draw_with(streams_of[4], (TOKENS, D), 1.0, 6.0, ((0, 8),), (0, 1, 8, 2.0))
    return dict(qkv=qkv, short_filter=short_filter, long_filter=long_filter, out_weight=out_weight, out_grad=out_grad)


def causal_conv(extended, lag_taps):
    n_taps = lag_taps.shape[0]
    n_out = extended.shape[0] - n_taps + 1

    def step(lag, total):
        window = lax.dynamic_slice_in_dim(extended, n_taps - 1 - lag, n_out, 0)
        return total + lag_taps[lag] * window

    return lax.fori_loop(0, n_taps, step, jnp.zeros((n_out, extended.shape[1]), jnp.float32))


def reverse_conv(extended, lag_taps):
    n_taps = lag_taps.shape[0]
    n_out = extended.shape[0] - n_taps + 1

    def step(lag, total):
        window = lax.dynamic_slice_in_dim(extended, lag, n_out, 0)
        return total + lag_taps[lag] * window

    return lax.fori_loop(0, n_taps, step, jnp.zeros((n_out, extended.shape[1]), jnp.float32))


def lag_sums(extended, signal):
    n_out = signal.shape[0]
    n_taps = extended.shape[0] - n_out + 1

    def one_lag(lag):
        window = lax.dynamic_slice_in_dim(extended, n_taps - 1 - lag, n_out, 0)
        return jnp.sum(signal * window, axis=0)

    return lax.map(one_lag, jnp.arange(n_taps))


def reference(qkv, short_filter, long_filter, out_weight, out_grad):
    width = 3 * D
    short_taps = short_filter.reshape(SHORT, width)
    own_rows = qkv.astype(jnp.float32).reshape(TOKENS, width)
    extended = jnp.concatenate([jnp.zeros((SHORT - 1, width), jnp.float32), own_rows], axis=0)
    smoothed = causal_conv(extended, short_taps).reshape(TOKENS, 3, D)
    query_s = smoothed[:, 0]
    key_s = smoothed[:, 1]
    value_s = smoothed[:, 2]
    product = (key_s * value_s).astype(jnp.bfloat16)
    long_taps = lax.optimization_barrier(long_filter.astype(jnp.bfloat16)).astype(jnp.float32)
    lagged = jnp.concatenate([jnp.zeros((LONG - 1, D), jnp.float32), product.astype(jnp.float32)], axis=0)
    long_out = causal_conv(lagged, long_taps)
    mixed = (query_s * long_out).astype(jnp.bfloat16)
    per_group = D // N_TENSOR
    summed = jnp.zeros((TOKENS, D), jnp.float32)
    for member in range(N_TENSOR):
        piece = jnp.dot(mixed[:, member * per_group:(member + 1) * per_group], out_weight[member * per_group:(member + 1) * per_group], preferred_element_type=jnp.float32).astype(jnp.bfloat16)
        piece = lax.optimization_barrier(piece)
        summed = summed + piece.astype(jnp.float32)
    output = summed.astype(jnp.bfloat16)
    mixed_grad = jnp.dot(out_grad, out_weight.T, preferred_element_type=jnp.float32)
    weight_grad = jnp.dot(out_grad.T, mixed, preferred_element_type=jnp.float32)
    long_out_grad = lax.optimization_barrier((mixed_grad * query_s).astype(jnp.bfloat16)).astype(jnp.float32)
    query_grad = mixed_grad * long_out
    padded_grad = jnp.concatenate([long_out_grad, jnp.zeros((LONG - 1, D), jnp.float32)], axis=0)
    product_grad = reverse_conv(padded_grad, long_taps)
    smoothed_grad = jnp.stack([query_grad, product_grad * value_s, product_grad * key_s], axis=1).reshape(TOKENS, width)
    padded_short = jnp.concatenate([smoothed_grad, jnp.zeros((SHORT - 1, width), jnp.float32)], axis=0)
    qkv_grad = reverse_conv(padded_short, short_taps).reshape(TOKENS, 3, D).astype(jnp.bfloat16)
    long_grad = lag_sums(lagged, long_out_grad)
    short_grad = lag_sums(extended, smoothed_grad).reshape(SHORT, 3, D)
    return (output, qkv_grad, long_grad, short_grad, weight_grad)
```

```python
import functools

import jax
import jax.numpy as jnp
import numpy as np
from jax import lax
from jax.experimental import pallas as pl
from jax.experimental.pallas import tpu as pltpu
from jax.sharding import PartitionSpec as P

BF = jnp.bfloat16
F32 = jnp.float32


def halves(array):
    high = np.asarray(array, np.float32).astype(jnp.bfloat16)
    low = (np.asarray(array, np.float32) - high.astype(np.float32)).astype(jnp.bfloat16)
    return high, low


def transforms(taps):
    n = 2 * taps
    angle = 2 * np.pi * np.outer(np.arange(taps) + 0.5, np.arange(n)) / n
    forward = np.concatenate([np.cos(angle), -np.sin(angle)], axis=0)
    inverse = np.concatenate([np.cos(angle), -np.sin(angle)], axis=0).T * (2.0 / n)
    return [jnp.asarray(part) for part in halves(forward) + halves(inverse)]


def mm(a, b):
    return jnp.dot(a, b, preferred_element_type=F32)


def split(value):
    high = value.astype(BF)
    return high, (value - high.astype(F32)).astype(BF)


def inverse_of(high_m, low_m, value):
    high, low = split(value)
    return mm(high_m, high) + (mm(high_m, low) + mm(low_m, high))


def times(a, b, n, conj):
    ar, ai, br, bi = a[:n], a[n:], b[:n], b[n:]
    if conj:
        return jnp.concatenate([ar * br + ai * bi, ai * br - ar * bi], axis=0)
    return jnp.concatenate([ar * br - ai * bi, ar * bi + ai * br], axis=0)


def first_kernel(n, pad, s, og, w, qkv, halo, short, longf, fh, fl, ih, il,
                 mixed, g_out, dq_out, ks_out, vs_out, lg, ext, prod, spec):
    rows = qkv.shape[1]
    top = n + pad
    for k in range(3):
        ext[k, 0:top, :] = halo[k].astype(F32)
        ext[k, top:, :] = qkv[k].astype(F32)
    h = longf[...].astype(BF)
    spec[...] = mm(fh[:, :n], h) + mm(fl[:, :n], h)
    lg[...] = jnp.zeros_like(lg)

    def smooth(k, e):
        window = ext[k, pl.ds(e, n + pad), :]
        total = short[k, 0:1, :] * window[pad:]
        for j in range(1, s):
            total = total + short[k, j:j + 1, :] * window[pad - j:pad - j + n]
        return total

    prod[0:n, :] = (smooth(1, 0) * smooth(2, 0)).astype(BF)

    def step(c, total):
        t = pl.multiple_of(c * n, n)
        e = pl.multiple_of(c * n + n, n)
        ks = smooth(1, e)
        vs = smooth(2, e)
        ks_out[pl.ds(t, n), :] = ks
        vs_out[pl.ds(t, n), :] = vs
        prod[pl.ds(e, n), :] = (ks * vs).astype(BF)
        qs = smooth(0, e)
        mg = lax.dot_general(og[pl.ds(t, n), :], w[...], (((1,), (1,)), ((), ())), preferred_element_type=F32)
        window = prod[pl.ds(t, 2 * n), :]
        x = mm(fh[...], window) + mm(fl[...], window)
        y = inverse_of(ih[n:, :], il[n:, :], times(x, spec[...], n, False))
        mixed[pl.ds(t, n), :] = (qs * y).astype(BF)
        g = (mg * qs).astype(BF)
        g_out[pl.ds(t, n), :] = g
        dq_out[pl.ds(t, n), :] = mg * y
        gs = mm(fh[:, n:], g) + mm(fl[:, n:], g)
        return total + times(gs, x, n, True)

    total = lax.fori_loop(0, rows // n, step, jnp.zeros((2 * n, w.shape[0]), F32))
    lg[...] = inverse_of(ih[:n, :], il[:n, :], total)


def second_kernel(n, pad, s, g, tail, dq, ks, vs, qkv, halo, short, longf, fh, fl, ih, il,
                  grad, sg, ext, gext, spec, sums):
    rows = qkv.shape[1]
    for k in range(3):
        ext[k, 0:pad, :] = halo[k, n:n + pad, :].astype(F32)
        ext[k, pad:, :] = qkv[k].astype(F32)
    gext[0:rows, :] = g[...]
    gext[rows:rows + n + 16, :] = tail[0:n + 16, :]
    gext[rows + n + 16:, :] = jnp.zeros((n - 16, g.shape[1]), BF)
    h = longf[...].astype(BF)
    spec[...] = mm(fh[:, :n], h) + mm(fl[:, :n], h)
    sums[...] = jnp.zeros_like(sums)

    def long_back(t):
        window = gext[pl.ds(t, 2 * n), :]
        x = mm(fh[...], window) + mm(fl[...], window)
        return inverse_of(ih[:n, :], il[:n, :], times(x, spec[...], n, True))

    pg = long_back(rows)[:pad]
    heads = (
        tail[n + 16:n + 16 + pad, :].astype(F32),
        pg * tail[n + 48:n + 48 + pad, :].astype(F32),
        pg * tail[n + 32:n + 32 + pad, :].astype(F32),
    )

    def step(i, heads):
        t = pl.multiple_of(rows - n - i * n, n)
        pg = long_back(t)
        owns = (dq[pl.ds(t, n), :], pg * vs[pl.ds(t, n), :], pg * ks[pl.ds(t, n), :])
        for k in range(3):
            own = owns[k]
            window = jnp.concatenate([own, heads[k]], axis=0)
            raw = ext[k, pl.ds(t, n + pad), :]
            total = short[k, 0:1, :] * own
            for j in range(s):
                if j:
                    total = total + short[k, j:j + 1, :] * window[j:j + n]
                term = own * raw[pad - j:pad - j + n]
                sums[k, j] += jnp.sum(term.reshape(n // 8, 8, term.shape[1]), axis=0)
            grad[k, pl.ds(t, n), :] = total.astype(BF)
        return tuple(own[:pad] for own in owns)

    lax.fori_loop(0, rows // n, step, heads)
    sg[...] = jnp.sum(sums[...], axis=2)


def shifted(value, axis, steps):
    count = lax.axis_size(axis)
    leading, last = (max(0, -steps), min(count, count - steps))
    return lax.ppermute(value, axis, [(source, source + steps) for source in range(leading, last)])


def shards(qkv, short_filter, long_filter, out_weight, out_grad):
    rows, _, chans = qkv.shape
    n, s, pad = long_filter.shape[0], short_filter.shape[0], 8
    feats = out_weight.shape[1]
    cb = 256
    streams = jnp.transpose(qkv, (1, 0, 2))
    short = jnp.transpose(short_filter, (1, 0, 2))
    halo = shifted(streams[:, rows - n - pad:], "context", 1)
    matrices = transforms(n)

    def by_chan(*lead):
        zeros = (0,) * len(lead)
        return pl.BlockSpec(lead + (cb,), lambda i: zeros + (i,))

    def whole(shape):
        zeros = (0,) * len(shape)
        return pl.BlockSpec(shape, lambda i: zeros)

    mats = [whole((2 * n, 2 * n))] * 4
    top = n + pad
    conv_flops = 40 * rows * n * chans
    params = pltpu.CompilerParams(vmem_limit_bytes=56 * 2**20)
    mixed, g, dq, ks, vs, long_local = pl.pallas_call(
        functools.partial(first_kernel, n, pad, s),
        grid=(chans // cb,),
        out_shape=[
            jax.ShapeDtypeStruct((rows, chans), BF),
            jax.ShapeDtypeStruct((rows, chans), BF),
            jax.ShapeDtypeStruct((rows, chans), F32),
            jax.ShapeDtypeStruct((rows, chans), F32),
            jax.ShapeDtypeStruct((rows, chans), F32),
            jax.ShapeDtypeStruct((n, chans), F32),
        ],
        in_specs=[
            whole((rows, feats)),
            pl.BlockSpec((cb, feats), lambda i: (i, 0)),
            by_chan(3, rows),
            by_chan(3, top),
            by_chan(3, s),
            by_chan(n),
        ] + mats,
        out_specs=[by_chan(rows)] * 5 + [by_chan(n)],
        scratch_shapes=[
            pltpu.VMEM((3, rows + top, cb), F32),
            pltpu.VMEM((rows + n, cb), BF),
            pltpu.VMEM((2 * n, cb), F32),
        ],
        compiler_params=params,
        cost_estimate=pl.CostEstimate(flops=2 * rows * chans * feats + conv_flops, bytes_accessed=20 * 2**20, transcendentals=0),
        name="forward",
    )(out_grad, out_weight, streams, halo, short, long_filter, *matrices)
    head = jnp.concatenate([g[:n + 16]] + [part[:16].astype(BF) for part in (dq, ks, vs)], axis=0)
    tail = shifted(head, "context", -1)
    partial_value = jnp.dot(mixed, out_weight, preferred_element_type=F32).astype(BF)
    output = lax.psum(partial_value, "tensor")
    weight_local = lax.dot_general(
        out_grad, mixed, (((0,), (0,)), ((), ())), preferred_element_type=F32
    ).astype(BF)
    weight_grad = lax.psum_scatter(weight_local, "context", scatter_dimension=0, tiled=True).astype(F32)
    g, tail, _ = lax.optimization_barrier((g, tail, weight_local))
    grad, short_local = pl.pallas_call(
        functools.partial(second_kernel, n, pad, s),
        grid=(chans // cb,),
        out_shape=[
            jax.ShapeDtypeStruct((3, rows, chans), BF),
            jax.ShapeDtypeStruct((3, s, chans), F32),
        ],
        in_specs=[by_chan(rows), by_chan(n + 64)] + [by_chan(rows)] * 3 + [
            by_chan(3, rows),
            by_chan(3, top),
            by_chan(3, s),
            by_chan(n),
        ] + mats,
        out_specs=[by_chan(3, rows), by_chan(3, s)],
        scratch_shapes=[
            pltpu.VMEM((3, rows + pad, cb), F32),
            pltpu.VMEM((rows + 2 * n, cb), BF),
            pltpu.VMEM((2 * n, cb), F32),
            pltpu.VMEM((3, s, 8, cb), F32),
        ],
        compiler_params=params,
        cost_estimate=pl.CostEstimate(flops=conv_flops * 4, bytes_accessed=20 * 2**20, transcendentals=0),
        name="backward",
    )(g, tail, dq, ks, vs, streams, halo, short, long_filter, *matrices)
    filters = jnp.concatenate([long_local, short_local.reshape(3 * s, chans)], axis=0)
    filters = lax.psum(filters, "context")
    long_grad = filters[:n]
    short_grad = jnp.transpose(filters[n:].reshape(3, s, chans), (1, 0, 2))
    return output, jnp.transpose(grad, (1, 0, 2)), long_grad, short_grad, weight_grad


def solution(mesh):
    in_specs = (
        P("context", None, "tensor"),
        P(None, None, "tensor"),
        P(None, "tensor"),
        P("tensor", None),
        P("context", None),
    )
    out_specs = (
        P("context", None),
        P("context", None, "tensor"),
        P(None, "tensor"),
        P(None, None, "tensor"),
        P("context", "tensor"),
    )
    return jax.shard_map(shards, mesh=mesh, in_specs=in_specs, out_specs=out_specs, check_vma=False)
```

```python
import functools

import jax
import jax.numpy as jnp
import numpy as np
from jax import lax
from jax.experimental import pallas as pl
from jax.experimental.pallas import tpu as pltpu
from jax.sharding import PartitionSpec as P

BF = jnp.bfloat16
F32 = jnp.float32


def halves(array):
    high = np.asarray(array, np.float32).astype(jnp.bfloat16)
    low = (np.asarray(array, np.float32) - high.astype(np.float32)).astype(jnp.bfloat16)
    return high, low


def transforms(taps):
    n = 2 * taps
    angle = 2 * np.pi * np.outer(np.arange(taps) + 0.5, np.arange(n)) / n
    forward = np.concatenate([np.cos(angle), -np.sin(angle)], axis=0)
    inverse = np.concatenate([np.cos(angle), -np.sin(angle)], axis=0).T * (2.0 / n)
    return [jnp.asarray(part) for part in halves(forward) + halves(inverse)]


def mm(a, b):
    return jnp.dot(a, b, preferred_element_type=F32)


def split(value):
    high = value.astype(BF)
    return high, (value - high.astype(F32)).astype(BF)


def inverse_of(high_m, low_m, value):
    high, low = split(value)
    return mm(high_m, high) + (mm(high_m, low) + mm(low_m, high))


def times(a, b, n, conj):
    ar, ai, br, bi = a[:n], a[n:], b[:n], b[n:]
    if conj:
        return jnp.concatenate([ar * br + ai * bi, ai * br - ar * bi], axis=0)
    return jnp.concatenate([ar * br - ai * bi, ar * bi + ai * br], axis=0)


def first_kernel(n, pad, s, og, w, qkv, halo, short, longf, fh, fl, ih, il,
                 mixed, g_out, dq_out, ks_out, vs_out, lg, ext, prod, spec):
    rows = qkv.shape[1]
    top = n + pad
    for k in range(3):
        ext[k, 0:top, :] = halo[k].astype(F32)
        ext[k, top:, :] = qkv[k].astype(F32)
    h = longf[...].astype(BF)
    spec[...] = mm(fh[:, :n], h) + mm(fl[:, :n], h)
    lg[...] = jnp.zeros_like(lg)

    def smooth(k, e):
        window = ext[k, pl.ds(e, n + pad), :]
        total = short[k, 0:1, :] * window[pad:]
        for j in range(1, s):
            total = total + short[k, j:j + 1, :] * window[pad - j:pad - j + n]
        return total

    prod[0:n, :] = (smooth(1, 0) * smooth(2, 0)).astype(BF)

    def step(c, total):
        t = pl.multiple_of(c * n, n)
        e = pl.multiple_of(c * n + n, n)
        ks = smooth(1, e)
        vs = smooth(2, e)
        ks_out[pl.ds(t, n), :] = ks
        vs_out[pl.ds(t, n), :] = vs
        prod[pl.ds(e, n), :] = (ks * vs).astype(BF)
        qs = smooth(0, e)
        mg = lax.dot_general(og[pl.ds(t, n), :], w[...], (((1,), (1,)), ((), ())), preferred_element_type=F32)
        window = prod[pl.ds(t, 2 * n), :]
        x = mm(fh[...], window) + mm(fl[...], window)
        y = inverse_of(ih[n:, :], il[n:, :], times(x, spec[...], n, False))
        mixed[pl.ds(t, n), :] = (qs * y).astype(BF)
        g = (mg * qs).astype(BF)
        g_out[pl.ds(t, n), :] = g
        dq_out[pl.ds(t, n), :] = mg * y
        gs = mm(fh[:, n:], g) + mm(fl[:, n:], g)
        return total + times(gs, x, n, True)

    total = lax.fori_loop(0, rows // n, step, jnp.zeros((2 * n, w.shape[0]), F32))
    lg[...] = inverse_of(ih[:n, :], il[:n, :], total)


def second_kernel(n, pad, s, g, tail, dq, ks, vs, qkv, halo, short, longf, fh, fl, ih, il,
                  grad, sg, ext, gext, spec, sums):
    rows = qkv.shape[1]
    for k in range(3):
        ext[k, 0:pad, :] = halo[k, n:n + pad, :].astype(F32)
        ext[k, pad:, :] = qkv[k].astype(F32)
    gext[0:rows, :] = g[...]
    gext[rows:rows + n + 16, :] = tail[0:n + 16, :]
    gext[rows + n + 16:, :] = jnp.zeros((n - 16, g.shape[1]), BF)
    h = longf[...].astype(BF)
    spec[...] = mm(fh[:, :n], h) + mm(fl[:, :n], h)
    sums[...] = jnp.zeros_like(sums)

    def long_back(t):
        window = gext[pl.ds(t, 2 * n), :]
        x = mm(fh[...], window) + mm(fl[...], window)
        return inverse_of(ih[:n, :], il[:n, :], times(x, spec[...], n, True))

    pg = long_back(rows)[:pad]
    heads = (
        tail[n + 16:n + 16 + pad, :].astype(F32),
        pg * tail[n + 48:n + 48 + pad, :].astype(F32),
        pg * tail[n + 32:n + 32 + pad, :].astype(F32),
    )

    def step(i, heads):
        t = pl.multiple_of(rows - n - i * n, n)
        pg = long_back(t)
        owns = (dq[pl.ds(t, n), :], pg * vs[pl.ds(t, n), :], pg * ks[pl.ds(t, n), :])
        for k in range(3):
            own = owns[k]
            window = jnp.concatenate([own, heads[k]], axis=0)
            raw = ext[k, pl.ds(t, n + pad), :]
            total = short[k, 0:1, :] * own
            for j in range(s):
                if j:
                    total = total + short[k, j:j + 1, :] * window[j:j + n]
                term = own * raw[pad - j:pad - j + n]
                sums[k, j] += jnp.sum(term.reshape(n // 8, 8, term.shape[1]), axis=0)
            grad[k, pl.ds(t, n), :] = total.astype(BF)
        return tuple(own[:pad] for own in owns)

    lax.fori_loop(0, rows // n, step, heads)
    sg[...] = jnp.sum(sums[...], axis=2)


def shifted(value, axis, steps):
    count = lax.axis_size(axis)
    leading, last = (max(0, -steps), min(count, count - steps))
    return lax.ppermute(value, axis, [(source, source + steps) for source in range(leading, last)])


def sum_kernel(count, chunks, part, filt, out, total, near, mine, far, slots, sems, fsems):
    mesh_id = pl.DeviceIdType.MESH
    place = lax.axis_index("context")
    member = lax.axis_index("tensor")
    core = lax.rem(member, 2)
    sibling = (place, member + 1 - 2 * core)
    peer = (place, lax.rem(member + 2, 4))
    others = [lax.rem(place + d, count) for d in range(1, count)]
    half = part.shape[0] // 2
    size = half // chunks
    piece = filt.shape[0] // count

    barrier = pltpu.get_barrier_semaphore()
    for device in [sibling, peer] + [(other, member) for other in others]:
        pl.semaphore_signal(barrier, inc=1, device_id=device, device_id_type=mesh_id)
    pl.semaphore_wait(barrier, count + 1)

    def send(source, target, pair, index, device):
        copy = pltpu.make_async_remote_copy(
            src_ref=source, dst_ref=target, send_sem=pair.at[0, index], recv_sem=pair.at[1, index],
            device_id=device, device_id_type=mesh_id,
        )
        copy.start()
        return copy

    def own_rows(side, c):
        return pl.ds(pl.multiple_of(side * half + c * size, size), size)

    def rows_of(index):
        return pl.ds(pl.multiple_of(index * piece, piece), piece)

    first = [
        send(part.at[own_rows(1 - core, c)], near.at[c], sems, c, sibling) for c in range(chunks)
    ]
    gather = [
        send(filt.at[rows_of(other)], slots.at[d], fsems, d, (other, member)) for d, other in enumerate(others)
    ]
    second = []
    for c in range(chunks):
        first[c].wait_recv()
        mine[c] = (part[own_rows(core, c), :].astype(F32) + near[c].astype(F32)).astype(BF)
        second.append(send(mine.at[c], far.at[c], sems, chunks + c, peer))
    for copy in gather:
        copy.wait_recv()
    value = filt[rows_of(place), :]
    for d in range(count - 1):
        value = value + slots[d]
    total[rows_of(place), :] = value
    spread = [
        send(total.at[rows_of(place)], total.at[rows_of(place)], fsems, count - 1 + d, (other, member))
        for d, other in enumerate(others)
    ]
    third = []
    for c in range(chunks):
        second[c].wait_recv()
        out[own_rows(core, c), :] = (mine[c].astype(F32) + far[c].astype(F32)).astype(BF)
        third.append(send(out.at[own_rows(core, c)], out.at[own_rows(core, c)], sems, 2 * chunks + c, sibling))
    for copy in spread + third:
        copy.wait_recv()
    for copy in first + gather + second + spread + third:
        copy.wait_send()


def summed(partial_value, filters):
    rows, feats = partial_value.shape
    count = lax.axis_size("context")
    length, chans = filters.shape
    piece = -(-length // (8 * count)) * 8
    filters = jnp.concatenate([filters, jnp.zeros((piece * count - length, chans), F32)], axis=0)
    chunks = 4
    size = rows // 2 // chunks
    vmem = pl.BlockSpec(memory_space=pltpu.VMEM)
    return pl.pallas_call(
        functools.partial(sum_kernel, count, chunks),
        out_shape=[
            jax.ShapeDtypeStruct((rows, feats), BF),
            jax.ShapeDtypeStruct((piece * count, chans), F32),
        ],
        in_specs=[vmem, vmem],
        out_specs=[vmem, vmem],
        scratch_shapes=[pltpu.VMEM((chunks, size, feats), BF)] * 3 + [
            pltpu.VMEM((count - 1, piece, chans), F32),
            pltpu.SemaphoreType.DMA((2, 3 * chunks)),
            pltpu.SemaphoreType.DMA((2, 2 * (count - 1))),
        ],
        compiler_params=pltpu.CompilerParams(
            collective_id=0, has_side_effects=True, vmem_limit_bytes=40 * 2**20
        ),
        cost_estimate=pl.CostEstimate(flops=6 * rows * feats, bytes_accessed=100 * 2**20, transcendentals=0),
        name="sums",
    )(partial_value, filters)


def shards(qkv, short_filter, long_filter, out_weight, out_grad):
    rows, _, chans = qkv.shape
    n, s, pad = long_filter.shape[0], short_filter.shape[0], 8
    feats = out_weight.shape[1]
    cb = 256
    streams = jnp.transpose(qkv, (1, 0, 2))
    short = jnp.transpose(short_filter, (1, 0, 2))
    halo = shifted(streams[:, rows - n - pad:], "context", 1)
    matrices = transforms(n)

    def by_chan(*lead):
        zeros = (0,) * len(lead)
        return pl.BlockSpec(lead + (cb,), lambda i: zeros + (i,))

    def whole(shape):
        zeros = (0,) * len(shape)
        return pl.BlockSpec(shape, lambda i: zeros)

    mats = [whole((2 * n, 2 * n))] * 4
    top = n + pad
    conv_flops = 40 * rows * n * chans
    params = pltpu.CompilerParams(vmem_limit_bytes=56 * 2**20)
    mixed, g, dq, ks, vs, long_local = pl.pallas_call(
        functools.partial(first_kernel, n, pad, s),
        grid=(chans // cb,),
        out_shape=[
            jax.ShapeDtypeStruct((rows, chans), BF),
            jax.ShapeDtypeStruct((rows, chans), BF),
            jax.ShapeDtypeStruct((rows, chans), F32),
            jax.ShapeDtypeStruct((rows, chans), F32),
            jax.ShapeDtypeStruct((rows, chans), F32),
            jax.ShapeDtypeStruct((n, chans), F32),
        ],
        in_specs=[
            whole((rows, feats)),
            pl.BlockSpec((cb, feats), lambda i: (i, 0)),
            by_chan(3, rows),
            by_chan(3, top),
            by_chan(3, s),
            by_chan(n),
        ] + mats,
        out_specs=[by_chan(rows)] * 5 + [by_chan(n)],
        scratch_shapes=[
            pltpu.VMEM((3, rows + top, cb), F32),
            pltpu.VMEM((rows + n, cb), BF),
            pltpu.VMEM((2 * n, cb), F32),
        ],
        compiler_params=params,
        cost_estimate=pl.CostEstimate(flops=2 * rows * chans * feats + conv_flops, bytes_accessed=20 * 2**20, transcendentals=0),
        name="forward",
    )(out_grad, out_weight, streams, halo, short, long_filter, *matrices)
    head = jnp.concatenate([g[:n + 16]] + [part[:16].astype(BF) for part in (dq, ks, vs)], axis=0)
    tail = shifted(head, "context", -1)
    partial_value = jnp.dot(mixed, out_weight, preferred_element_type=F32).astype(BF)
    weight_local = lax.dot_general(
        out_grad, mixed, (((0,), (0,)), ((), ())), preferred_element_type=F32
    ).astype(BF)
    weight_grad = lax.psum_scatter(weight_local, "context", scatter_dimension=0, tiled=True).astype(F32)
    g, tail, _ = lax.optimization_barrier((g, tail, weight_local))
    grad, short_local = pl.pallas_call(
        functools.partial(second_kernel, n, pad, s),
        grid=(chans // cb,),
        out_shape=[
            jax.ShapeDtypeStruct((3, rows, chans), BF),
            jax.ShapeDtypeStruct((3, s, chans), F32),
        ],
        in_specs=[by_chan(rows), by_chan(n + 64)] + [by_chan(rows)] * 3 + [
            by_chan(3, rows),
            by_chan(3, top),
            by_chan(3, s),
            by_chan(n),
        ] + mats,
        out_specs=[by_chan(3, rows), by_chan(3, s)],
        scratch_shapes=[
            pltpu.VMEM((3, rows + pad, cb), F32),
            pltpu.VMEM((rows + 2 * n, cb), BF),
            pltpu.VMEM((2 * n, cb), F32),
            pltpu.VMEM((3, s, 8, cb), F32),
        ],
        compiler_params=params,
        cost_estimate=pl.CostEstimate(flops=conv_flops * 4, bytes_accessed=20 * 2**20, transcendentals=0),
        name="backward",
    )(g, tail, dq, ks, vs, streams, halo, short, long_filter, *matrices)
    filters = jnp.concatenate([long_local, short_local.reshape(3 * s, chans)], axis=0)
    output, filters = summed(partial_value, filters)
    long_grad = filters[:n]
    short_grad = jnp.transpose(filters[n:n + 3 * s].reshape(3, s, chans), (1, 0, 2))
    return output, jnp.transpose(grad, (1, 0, 2)), long_grad, short_grad, weight_grad


def solution(mesh):
    in_specs = (
        P("context", None, "tensor"),
        P(None, None, "tensor"),
        P(None, "tensor"),
        P("tensor", None),
        P("context", None),
    )
    out_specs = (
        P("context", None),
        P("context", None, "tensor"),
        P(None, "tensor"),
        P(None, None, "tensor"),
        P("context", "tensor"),
    )
    return jax.shard_map(shards, mesh=mesh, in_specs=in_specs, out_specs=out_specs, check_vma=False)
```

```python
import functools

import jax
import jax.numpy as jnp
import numpy as np
from jax import lax
from jax.experimental import pallas as pl
from jax.experimental.pallas import tpu as pltpu
from jax.sharding import PartitionSpec as P

BF = jnp.bfloat16
F32 = jnp.float32


def halves(array):
    high = np.asarray(array, np.float32).astype(jnp.bfloat16)
    low = (np.asarray(array, np.float32) - high.astype(np.float32)).astype(jnp.bfloat16)
    return high, low


def transforms(taps):
    n = 2 * taps
    angle = 2 * np.pi * np.outer(np.arange(taps) + 0.5, np.arange(n)) / n
    forward = np.concatenate([np.cos(angle), -np.sin(angle)], axis=0)
    inverse = np.concatenate([np.cos(angle), -np.sin(angle)], axis=0).T * (2.0 / n)
    return [jnp.asarray(part) for part in halves(forward) + halves(inverse)]


def mm(a, b):
    return jnp.dot(a, b, preferred_element_type=F32)


def split(value):
    high = value.astype(BF)
    return high, (value - high.astype(F32)).astype(BF)


def inverse_of(high_m, low_m, value):
    high, low = split(value)
    return mm(high_m, high) + (mm(high_m, low) + mm(low_m, high))


def times(a, b, n, conj):
    ar, ai, br, bi = a[:n], a[n:], b[:n], b[n:]
    if conj:
        return jnp.concatenate([ar * br + ai * bi, ai * br - ar * bi], axis=0)
    return jnp.concatenate([ar * br - ai * bi, ar * bi + ai * br], axis=0)


def first_kernel(n, pad, s, og, w, qkv, halo, short, longf, fh, fl, ih, il,
                 mixed, g_out, dq_out, ks_out, vs_out, lg, ext, prod, spec):
    rows = qkv.shape[1]
    top = n + pad
    for k in range(3):
        ext[k, 0:top, :] = halo[k].astype(F32)
        ext[k, top:, :] = qkv[k].astype(F32)
    h = longf[...].astype(BF)
    spec[...] = mm(fh[:, :n], h) + mm(fl[:, :n], h)
    lg[...] = jnp.zeros_like(lg)

    def smooth(k, e):
        window = ext[k, pl.ds(e, n + pad), :]
        total = short[k, 0:1, :] * window[pad:]
        for j in range(1, s):
            total = total + short[k, j:j + 1, :] * window[pad - j:pad - j + n]
        return total

    prod[0:n, :] = (smooth(1, 0) * smooth(2, 0)).astype(BF)

    def step(c, total):
        t = pl.multiple_of(c * n, n)
        e = pl.multiple_of(c * n + n, n)
        ks = smooth(1, e)
        vs = smooth(2, e)
        ks_out[pl.ds(t, n), :] = ks
        vs_out[pl.ds(t, n), :] = vs
        prod[pl.ds(e, n), :] = (ks * vs).astype(BF)
        qs = smooth(0, e)
        mg = lax.dot_general(og[pl.ds(t, n), :], w[...], (((1,), (1,)), ((), ())), preferred_element_type=F32)
        window = prod[pl.ds(t, 2 * n), :]
        x = mm(fh[...], window) + mm(fl[...], window)
        y = inverse_of(ih[n:, :], il[n:, :], times(x, spec[...], n, False))
        mixed[pl.ds(t, n), :] = (qs * y).astype(BF)
        g = (mg * qs).astype(BF)
        g_out[pl.ds(t, n), :] = g
        dq_out[pl.ds(t, n), :] = mg * y
        gs = mm(fh[:, n:], g) + mm(fl[:, n:], g)
        return total + times(gs, x, n, True)

    total = lax.fori_loop(0, rows // n, step, jnp.zeros((2 * n, w.shape[0]), F32))
    lg[...] = inverse_of(ih[:n, :], il[:n, :], total)


def second_kernel(n, pad, s, g, tail, dq, ks, vs, qkv, halo, short, longf, fh, fl, ih, il,
                  grad, sg, ext, gext, spec, sums):
    rows = qkv.shape[1]
    for k in range(3):
        ext[k, 0:pad, :] = halo[k, n:n + pad, :].astype(F32)
        ext[k, pad:, :] = qkv[k].astype(F32)
    gext[0:rows, :] = g[...]
    gext[rows:rows + n + 16, :] = tail[0:n + 16, :]
    gext[rows + n + 16:, :] = jnp.zeros((n - 16, g.shape[1]), BF)
    h = longf[...].astype(BF)
    spec[...] = mm(fh[:, :n], h) + mm(fl[:, :n], h)
    sums[...] = jnp.zeros_like(sums)

    def long_back(t):
        window = gext[pl.ds(t, 2 * n), :]
        x = mm(fh[...], window) + mm(fl[...], window)
        return inverse_of(ih[:n, :], il[:n, :], times(x, spec[...], n, True))

    pg = long_back(rows)[:pad]
    heads = (
        tail[n + 16:n + 16 + pad, :].astype(F32),
        pg * tail[n + 48:n + 48 + pad, :].astype(F32),
        pg * tail[n + 32:n + 32 + pad, :].astype(F32),
    )

    def step(i, heads):
        t = pl.multiple_of(rows - n - i * n, n)
        pg = long_back(t)
        owns = (dq[pl.ds(t, n), :], pg * vs[pl.ds(t, n), :], pg * ks[pl.ds(t, n), :])
        for k in range(3):
            own = owns[k]
            window = jnp.concatenate([own, heads[k]], axis=0)
            raw = ext[k, pl.ds(t, n + pad), :]
            total = short[k, 0:1, :] * own
            for j in range(s):
                if j:
                    total = total + short[k, j:j + 1, :] * window[j:j + n]
                term = own * raw[pad - j:pad - j + n]
                sums[k, j] += jnp.sum(term.reshape(n // 8, 8, term.shape[1]), axis=0)
            grad[k, pl.ds(t, n), :] = total.astype(BF)
        return tuple(own[:pad] for own in owns)

    lax.fori_loop(0, rows // n, step, heads)
    sg[...] = jnp.sum(sums[...], axis=2)


def shifted(value, axis, steps):
    count = lax.axis_size(axis)
    leading, last = (max(0, -steps), min(count, count - steps))
    return lax.ppermute(value, axis, [(source, source + steps) for source in range(leading, last)])


def sum_kernel(count, chunks, mine, far, filt, out, total, slots, sems, fsems):
    mesh_id = pl.DeviceIdType.MESH
    place = lax.axis_index("context")
    member = lax.axis_index("tensor")
    core = lax.rem(member, 2)
    sibling = (place, member + 1 - 2 * core)
    others = [lax.rem(place + d, count) for d in range(1, count)]
    half = mine.shape[0]
    size = half // chunks
    piece = filt.shape[0] // count

    barrier = pltpu.get_barrier_semaphore()
    for device in [sibling] + [(other, member) for other in others]:
        pl.semaphore_signal(barrier, inc=1, device_id=device, device_id_type=mesh_id)
    pl.semaphore_wait(barrier, count)

    def send(source, target, pair, index, device):
        copy = pltpu.make_async_remote_copy(
            src_ref=source, dst_ref=target, send_sem=pair.at[0, index], recv_sem=pair.at[1, index],
            device_id=device, device_id_type=mesh_id,
        )
        copy.start()
        return copy

    def own_rows(side, c):
        return pl.ds(pl.multiple_of(side * half + c * size, size), size)

    def rows_of(index):
        return pl.ds(pl.multiple_of(index * piece, piece), piece)

    gather = [
        send(filt.at[rows_of(other)], slots.at[d], fsems, d, (other, member)) for d, other in enumerate(others)
    ]
    third = []
    for c in range(chunks):
        out[own_rows(core, c), :] = (mine[pl.ds(c * size, size), :].astype(F32) + far[pl.ds(c * size, size), :].astype(F32)).astype(BF)
        third.append(send(out.at[own_rows(core, c)], out.at[own_rows(core, c)], sems, c, sibling))
    for copy in gather:
        copy.wait_recv()
    value = filt[rows_of(place), :]
    for d in range(count - 1):
        value = value + slots[d]
    total[rows_of(place), :] = value
    spread = [
        send(total.at[rows_of(place)], total.at[rows_of(place)], fsems, count - 1 + d, (other, member))
        for d, other in enumerate(others)
    ]
    for copy in spread + third:
        copy.wait_recv()
    for copy in gather + spread + third:
        copy.wait_send()


def summed(mine, far, filters):
    rows, feats = 2 * mine.shape[0], mine.shape[1]
    count = lax.axis_size("context")
    length, chans = filters.shape
    piece = -(-length // (8 * count)) * 8
    filters = jnp.concatenate([filters, jnp.zeros((piece * count - length, chans), F32)], axis=0)
    chunks = 4
    vmem = pl.BlockSpec(memory_space=pltpu.VMEM)
    return pl.pallas_call(
        functools.partial(sum_kernel, count, chunks),
        out_shape=[
            jax.ShapeDtypeStruct((rows, feats), BF),
            jax.ShapeDtypeStruct((piece * count, chans), F32),
        ],
        in_specs=[vmem] * 3,
        out_specs=[vmem, vmem],
        scratch_shapes=[
            pltpu.VMEM((count - 1, piece, chans), F32),
            pltpu.SemaphoreType.DMA((2, chunks)),
            pltpu.SemaphoreType.DMA((2, 2 * (count - 1))),
        ],
        compiler_params=pltpu.CompilerParams(
            collective_id=0, has_side_effects=True, vmem_limit_bytes=40 * 2**20
        ),
        cost_estimate=pl.CostEstimate(flops=6 * rows * feats, bytes_accessed=100 * 2**20, transcendentals=0),
        name="sums",
    )(mine, far, filters)


def shards(qkv, short_filter, long_filter, out_weight, out_grad):
    rows, _, chans = qkv.shape
    n, s, pad = long_filter.shape[0], short_filter.shape[0], 8
    feats = out_weight.shape[1]
    cb = 256
    streams = jnp.transpose(qkv, (1, 0, 2))
    short = jnp.transpose(short_filter, (1, 0, 2))
    halo = shifted(streams[:, rows - n - pad:], "context", 1)
    matrices = transforms(n)

    def by_chan(*lead):
        zeros = (0,) * len(lead)
        return pl.BlockSpec(lead + (cb,), lambda i: zeros + (i,))

    def whole(shape):
        zeros = (0,) * len(shape)
        return pl.BlockSpec(shape, lambda i: zeros)

    mats = [whole((2 * n, 2 * n))] * 4
    top = n + pad
    conv_flops = 40 * rows * n * chans
    params = pltpu.CompilerParams(vmem_limit_bytes=56 * 2**20)
    mixed, g, dq, ks, vs, long_local = pl.pallas_call(
        functools.partial(first_kernel, n, pad, s),
        grid=(chans // cb,),
        out_shape=[
            jax.ShapeDtypeStruct((rows, chans), BF),
            jax.ShapeDtypeStruct((rows, chans), BF),
            jax.ShapeDtypeStruct((rows, chans), F32),
            jax.ShapeDtypeStruct((rows, chans), F32),
            jax.ShapeDtypeStruct((rows, chans), F32),
            jax.ShapeDtypeStruct((n, chans), F32),
        ],
        in_specs=[
            whole((rows, feats)),
            pl.BlockSpec((cb, feats), lambda i: (i, 0)),
            by_chan(3, rows),
            by_chan(3, top),
            by_chan(3, s),
            by_chan(n),
        ] + mats,
        out_specs=[by_chan(rows)] * 5 + [by_chan(n)],
        scratch_shapes=[
            pltpu.VMEM((3, rows + top, cb), F32),
            pltpu.VMEM((rows + n, cb), BF),
            pltpu.VMEM((2 * n, cb), F32),
        ],
        compiler_params=params,
        cost_estimate=pl.CostEstimate(flops=2 * rows * chans * feats + conv_flops, bytes_accessed=20 * 2**20, transcendentals=0),
        name="forward",
    )(out_grad, out_weight, streams, halo, short, long_filter, *matrices)
    head = jnp.concatenate([g[:n + 16]] + [part[:16].astype(BF) for part in (dq, ks, vs)], axis=0)
    tail = shifted(head, "context", -1)
    partial_value = jnp.dot(mixed, out_weight, preferred_element_type=F32).astype(BF)
    weight_local = lax.dot_general(
        out_grad, mixed, (((0,), (0,)), ((), ())), preferred_element_type=F32
    ).astype(BF)
    weight_grad = lax.psum_scatter(weight_local, "context", scatter_dimension=0, tiled=True).astype(F32)
    core = lax.rem(lax.axis_index("tensor"), 2)
    half = rows // 2
    near = lax.ppermute(
        lax.dynamic_slice_in_dim(partial_value, (1 - core) * half, half, 0),
        "tensor", [(0, 1), (1, 0), (2, 3), (3, 2)],
    )
    own = lax.dynamic_slice_in_dim(partial_value, core * half, half, 0)
    mine = (own.astype(F32) + near.astype(F32)).astype(BF)
    mine, tail = lax.optimization_barrier((mine, tail))
    far = lax.ppermute(mine, "tensor", [(0, 2), (2, 0), (1, 3), (3, 1)])
    g, tail, _, _ = lax.optimization_barrier((g, tail, weight_local, mine))
    grad, short_local = pl.pallas_call(
        functools.partial(second_kernel, n, pad, s),
        grid=(chans // cb,),
        out_shape=[
            jax.ShapeDtypeStruct((3, rows, chans), BF),
            jax.ShapeDtypeStruct((3, s, chans), F32),
        ],
        in_specs=[by_chan(rows), by_chan(n + 64)] + [by_chan(rows)] * 3 + [
            by_chan(3, rows),
            by_chan(3, top),
            by_chan(3, s),
            by_chan(n),
        ] + mats,
        out_specs=[by_chan(3, rows), by_chan(3, s)],
        scratch_shapes=[
            pltpu.VMEM((3, rows + pad, cb), F32),
            pltpu.VMEM((rows + 2 * n, cb), BF),
            pltpu.VMEM((2 * n, cb), F32),
            pltpu.VMEM((3, s, 8, cb), F32),
        ],
        compiler_params=params,
        cost_estimate=pl.CostEstimate(flops=conv_flops * 4, bytes_accessed=20 * 2**20, transcendentals=0),
        name="backward",
    )(g, tail, dq, ks, vs, streams, halo, short, long_filter, *matrices)
    filters = jnp.concatenate([long_local, short_local.reshape(3 * s, chans)], axis=0)
    output, filters = summed(mine, far, filters)
    long_grad = filters[:n]
    short_grad = jnp.transpose(filters[n:n + 3 * s].reshape(3, s, chans), (1, 0, 2))
    return output, jnp.transpose(grad, (1, 0, 2)), long_grad, short_grad, weight_grad


def solution(mesh):
    in_specs = (
        P("context", None, "tensor"),
        P(None, None, "tensor"),
        P(None, "tensor"),
        P("tensor", None),
        P("context", None),
    )
    out_specs = (
        P("context", None),
        P("context", None, "tensor"),
        P(None, "tensor"),
        P(None, None, "tensor"),
        P("context", "tensor"),
    )
    return jax.shard_map(shards, mesh=mesh, in_specs=in_specs, out_specs=out_specs, check_vma=False)
```
